128 devices in a mesh: grp: 2 (over x_lo), sx: 16 (over z, x_hi, core), sy: 4 (over y).
Axes of the slice: x: 4 (x_hi: 2, x_lo: 2; x = x_hi * 2 + x_lo), y: 4, z: 4, core: 2. Of those that a mesh axis runs over, the one named last changes fastest.
Arguments:
- component_grids: float32 [4, 128, 4, 4, 16, 8, 128], P('grp', 'sx', None, None, 'sy'), may hold values from -6 to 6
- levels: int32 [4, 6], P('grp'), may hold values from 2 to 7, as said below
- coefficients: int32 [4], P('grp'), may hold values from -2 to 1, as said below
Outputs:
- combined_grids: float32 [4, 128, 4, 4, 16, 8, 128], P('grp', 'sx', None, None, 'sy')
The draws below stay inside these ranges and needn't reach their ends.
Inputs may be any that keep to these rules, and one draw needn't show every extreme that they name: `levels`: every grid has the full level in dimensions two, three and five. In dimensions one, four and six one grid is one below the full level in all three; each of the other three grids has the full level in exactly one of these three dimensions, a different one for each, and is one below it in the other two. `coefficients`: the coefficient is -2 for the grid that is below the full level in dimensions one, four and six, and 1 for every other grid.
All inputs are finite; a program needn't handle non-finite values.
Results may differ from the reference program's by a relative error of at most 0.0003.
Values sent between devices are 32-bit elements; how exact they have to be, the bound alone decides.
No kernel may reach another device: no remote copies, remote signals or barrier semaphores. Data moves between devices by JAX's collectives and lax.ppermute only.
A program may use at most 128 MiB of HBM per device.

```python
import jax
import jax.numpy as jnp
import numpy as np

LV1 = 7
LV2 = 2
LV3 = 2
LV4 = 4
LV5 = 3
LV6 = 7
N1 = 128
N2 = 4
N3 = 4
N4 = 16
N5 = 8
N6 = 128
GRIDS = 4


def grid_roles(key):
    return jax.random.permutation(key, GRIDS).astype(jnp.int32)


def draw_levels(key, part):
    roles = grid_roles(key)
    fulls = jnp.array([LV1, LV2, LV3, LV4, LV5, LV6], jnp.int32)
    column_index = jnp.arange(6, dtype=jnp.int32)[None, :]
    varying = (column_index == 0) | (column_index == 3) | (column_index == 5)
    targets = jnp.array([-1, 0, 3, 5], jnp.int32)[roles]
    lowered = varying & (column_index != targets[:, None])
    return (fulls[None, :] - lowered.astype(jnp.int32)).astype(jnp.int32)


def draw_coefficients(key, part):
    roles = grid_roles(key)
    return jnp.where(roles == 0, -2, 1).astype(jnp.int32)


def block_scale(key, dims, cuts, least, high):
    factor_of, own = 1.0, jax.random.fold_in(key, 6)
    for dim, parts in cuts:
        draws = jnp.exp(jax.random.uniform(jax.random.fold_in(own, dim), (parts,), jnp.float32, least / len(cuts), high / len(cuts)))
        factor_of = factor_of * jnp.repeat(draws, dims[dim] // parts).reshape([-1 if axis == dim else 1 for axis in range(len(dims))])
    return factor_of


def noise(own_key, dims, spread, limit, pieces=(), kind=jnp.bfloat16):
    result = spread * jax.random.normal(own_key, dims, jnp.float32)
    if pieces:
        result = result * block_scale(own_key, dims, pieces, -0.22, 0.18)
    return jnp.clip(result, -limit, limit).astype(kind)


def setup_inputs(seed: int = 0) -> dict:
    key_of = jax.random.split(jax.random.key(seed), 4)
    return {
        "component_grids": noise(key_of[0], (GRIDS, N1, N2, N3, N4, N5, N6), 1.0, 6.0, ((0, 2), (1, 16), (4, 4)), jnp.float32),
        "levels": draw_levels(jax.random.fold_in(key_of[3], 71), 0),
        "coefficients": draw_coefficients(jax.random.fold_in(key_of[3], 71), 0),
    }


def hierarchize_axis(current, target_axis):
    length = current.shape[target_axis]
    position = np.arange(length)
    low_bit = position & -position
    lower_index = jnp.asarray((position - low_bit) % length, jnp.int32)
    upper_index = jnp.asarray((position + low_bit) % length, jnp.int32)
    layout = [1] * current.ndim
    layout[target_axis] = length
    factor = jnp.asarray(np.where(position > 0, 0.5, 0.0), jnp.float32).reshape(layout)
    parents = jnp.take(current, lower_index, axis=target_axis) + jnp.take(current, upper_index, axis=target_axis)
    return current - factor * parents


def dehierarchize_axis(current, target_axis):
    length = current.shape[target_axis]
    position = np.arange(length)
    low_bit = position & -position
    layout = [1] * current.ndim
    layout[target_axis] = length
    stride = length // 2
    while stride >= 1:
        lower_index = jnp.asarray((position - stride) % length, jnp.int32)
        upper_index = jnp.asarray((position + stride) % length, jnp.int32)
        factor = jnp.asarray(np.where(low_bit == stride, 0.5, 0.0), jnp.float32).reshape(layout)
        parents = jnp.take(current, lower_index, axis=target_axis) + jnp.take(current, upper_index, axis=target_axis)
        current = current + factor * parents
        stride = stride // 2
    return current


def transform(current, operation):
    for target_axis in range(6):
        current = operation(current, target_axis)
    return current


def grid_mask(level_row):
    totals = [N1, N2, N3, N4, N5, N6]
    fulls = [LV1, LV2, LV3, LV4, LV5, LV6]
    selector = jnp.ones((1, 1, 1, 1, 1, 1), jnp.float32)
    for dimension in range(6):
        spacing = jnp.left_shift(jnp.int32(1), fulls[dimension] - level_row[dimension])
        position_index = jnp.arange(totals[dimension], dtype=jnp.int32)
        kept_points = (position_index % spacing == 0).astype(jnp.float32)
        layout = [1, 1, 1, 1, 1, 1]
        layout[dimension] = totals[dimension]
        selector = selector * kept_points.reshape(layout)
    return selector


def reference(component_grids, levels, coefficients):
    selectors = [grid_mask(levels[member]) for member in range(GRIDS)]
    combined = jnp.zeros(component_grids.shape[1:], jnp.float32)
    for member in range(GRIDS):
        surplus = transform(component_grids[member], hierarchize_axis)
        combined = combined + coefficients[member].astype(jnp.float32) * selectors[member] * surplus
    outputs = [transform(selectors[member] * combined, dehierarchize_axis) for member in range(GRIDS)]
    return jnp.stack(outputs)
```

```python
import jax
import jax.numpy as jnp
from jax import lax
from jax.experimental import pallas as pl
from jax.experimental.pallas import tpu as pltpu
from jax.sharding import PartitionSpec as P

AXES = ("grp", "sx", "sy")
FULL = (7, 4, 7)
VARYING = (0, 3, 5)
TILE = (8, 128)
F32 = jnp.float32


def even_lanes():
    return (lax.broadcasted_iota(jnp.int32, TILE, 1) & 1) == 0


def ahead(x, lanes=1):
    return pltpu.roll(x, 128 - lanes, 1)


def behind(x):
    return pltpu.roll(x, 1, 1)


def pack(even, a, b):
    return jnp.where(even, a, behind(b))


def pack_odd(even, a, b):
    return jnp.where(even, ahead(a), b)


def along_lanes(x):
    return x - 0.5 * (behind(x) + ahead(x))


def expand(even, p, odd=None):
    following = ahead(p)
    first, second = 0.5 * (behind(p) + following), 0.5 * (p + ahead(p, 2))
    if odd is not None:
        first, second = first + behind(odd), second + odd
    return jnp.where(even, p, first), jnp.where(even, following, second)


def mean_of(x, y):
    return 0.5 * (x + y)


def fine_in(levels, g, which):
    return levels[g, VARYING[which]] == FULL[which]


def weight_of(coefficients, g):
    return coefficients[g].astype(F32)


def first_kernel(
    far_levels, far_coefficients, u, sums, over_sy, coarse, odd, levels, coefficients, sem
):
    scalars = [
        pltpu.make_async_copy(far_levels, levels, sem.at[0]),
        pltpu.make_async_copy(far_coefficients, coefficients, sem.at[1]),
    ]
    nodal = [
        pltpu.make_async_copy(u.at[g, :, 0, :, :, n, 0], coarse.at[g, n], sem.at[2 + 2 * g + n])
        for g in range(2)
        for n in range(2)
    ]
    for copy in scalars + nodal:
        copy.start()
    for copy in scalars:
        copy.wait()
    finer = []
    for g in range(2):
        one = fine_in(levels, g, 0).astype(jnp.int32)
        four = fine_in(levels, g, 1).astype(jnp.int32)
        for n in range(2):
            copy = pltpu.make_async_copy(
                u.at[g, :, one, :, :, n, four], odd.at[g, n], sem.at[6 + 2 * g + n]
            )
            copy.start()
            finer.append(copy)
    even = even_lanes()
    weights = [weight_of(coefficients, g) for g in range(2)]
    for copy in nodal:
        copy.wait()

    @pl.loop(0, 4)
    def _(m):
        for n in range(2):
            for q in range(8):
                a, b = (
                    weights[0] * coarse[0, n, m, h, q] + weights[1] * coarse[1, n, m, h, q]
                    for h in range(2)
                )
                sums[m, n, q] = pack(even, a, b)

    for copy in finer:
        copy.wait()
    for g in range(2):
        one, six = fine_in(levels, g, 0), fine_in(levels, g, 2)

        @pl.when(one)
        def _():
            for m in range(4):
                for q in range(8):
                    halves = []
                    for h in range(2):
                        parents = coarse[g, 0, m, h, q]
                        if m < 3:
                            parents = parents + coarse[g, 0, m + 1, h, q]
                        halves.append(weights[g] * (odd[g, 0, m, h, q] - 0.5 * parents))
                    over_sy[g, m, q] = pack(even, *halves)

        @pl.when(six)
        def _():
            for m in range(4):
                for q in range(8):
                    halves = [weights[g] * along_lanes(coarse[g, 0, m, h, q]) for h in range(2)]
                    over_sy[g, m, q] = pack_odd(even, *halves)

        @pl.when(jnp.logical_not(one | six))
        def _():
            for m in range(4):
                for q in range(8):
                    halves = [weights[g] * coarse[g, 0, m, h, q] for h in range(2)]
                    over_sy[g, m, q] = pack(even, *halves)


def second_kernel(levels, coefficients, coarse, odd, fine, over_sx, corner):
    even = even_lanes()
    for g in range(2):
        weight = weight_of(coefficients, g)
        one, four, six = (fine_in(levels, g, which) for which in range(3))

        def nodal(n, m, q):
            return pack(even, *[weight * coarse[g, n, m, h, q] for h in range(2)])

        def each(body):
            @pl.loop(0, 4)
            def _(block):
                for k in range(2):
                    body(2 * block + k)

        @pl.when(one)
        def _():
            def body(q):
                for n in range(2):
                    for m in range(4):
                        halves = []
                        for h in range(2):
                            parents = coarse[g, n, m, h, q]
                            if m < 3:
                                parents = parents + coarse[g, n, m + 1, h, q]
                            halves.append(weight * (odd[g, n, m, h, q] - 0.5 * parents))
                        fine[g, m, n, q] = pack(even, *halves)
                    edge = nodal(n, 0, q)
                    over_sx[g, n, q] = edge
                    if n == 0:
                        corner[g, q] = edge

            each(body)

        @pl.when(four)
        def _():
            def body(q):
                for n in range(2):
                    for m in range(4):
                        halves = []
                        for h in range(2):
                            parents = coarse[g, n, m, h, q]
                            if n < 1:
                                parents = parents + coarse[g, n + 1, m, h, q]
                            halves.append(weight * (odd[g, n, m, h, q] - 0.5 * parents))
                        packed = pack(even, *halves)
                        fine[g, m, n, q] = packed
                        if m == 0:
                            over_sx[g, n, q] = packed
                corner[g, q] = nodal(0, 0, q)

            each(body)

        @pl.when(six)
        def _():
            def body(q):
                for n in range(2):
                    for m in range(4):
                        halves = [weight * along_lanes(coarse[g, n, m, h, q]) for h in range(2)]
                        packed = pack_odd(even, *halves)
                        fine[g, m, n, q] = packed
                        if m == 0:
                            over_sx[g, n, q] = packed
                            if n == 0:
                                corner[g, q] = packed

            each(body)

        @pl.when(jnp.logical_not(one | four | six))
        def _():
            over_sx[g] = jnp.zeros(over_sx.shape[1:], F32)
            corner[g] = jnp.zeros(corner.shape[1:], F32)


def third_kernel(sums, other, over_sx, corner, to_sy, to_sx, to_corner):
    for m in range(4):
        to_sy[m] = sums[m, 0] + other[m, 0]
    to_sx[0] = to_sy[0]
    to_sx[1] = sums[0, 1] + other[0, 1]
    to_corner[0] = to_sy[0]
    for g in range(2):
        for n in range(2):
            to_sx[2 + 2 * g + n] = over_sx[g, n]
        to_corner[1 + g] = corner[g]


def remembered(rule):
    seen = {}

    def value(i, j):
        if (i, j) not in seen:
            seen[i, j] = rule(value, i, j)
        return seen[i, j]

    return value


def mean_pair(x, y):
    return tuple(mean_of(a, b) for a, b in zip(x, y))


def along_one(value, i, j):
    return value(i - 1, j), value(i + 1, j)


def along_four(value, i, j):
    return value(i, j - 1), value(i, j + 1)


def emit(points, late, levels, g, columns, nodal, fine_one, fine_four, fine_six, put, done):
    even = even_lanes()
    one, four, six = (fine_in(levels, g, which) for which in range(3))

    def both(leaf, mean):
        def rule(value, i, j):
            if i % 2:
                return mean(*along_one(value, i, j))
            if j % 2:
                return mean(*along_four(value, i, j))
            return leaf(i // 2, j // 2)

        return remembered(rule)

    def each(row_of):
        @pl.loop(0, 8 // columns)
        def _(block):
            for k in range(columns):
                q = block * columns + k
                row = row_of(q, both(lambda m, n: nodal(q, m, n), mean_of))
                for i, j in points:
                    put(q, i, j, row(i, j))
                done(q)

    @pl.when(one)
    def _():
        def row_of(q, base):
            def extra(value, i, j):
                if j % 2:
                    return mean_of(*along_four(value, i, j))
                return fine_one(q, i // 2, j // 2)

            extra = remembered(extra)

            def rule(value, i, j):
                if j % 2 and not late:
                    return mean_pair(*along_four(value, i, j))
                return expand(even, base(i, j) + extra(i, j) if i % 2 else base(i, j))

            return remembered(rule)

        each(row_of)

    @pl.when(four)
    def _():
        def row_of(q, base):
            def extra(value, i, j):
                if i % 2:
                    return mean_of(*along_one(value, i, j))
                return fine_four(q, i // 2, j // 2)

            extra = remembered(extra)

            def rule(value, i, j):
                if i % 2 and not late:
                    return mean_pair(*along_one(value, i, j))
                return expand(even, base(i, j) + extra(i, j) if j % 2 else base(i, j))

            return remembered(rule)

        each(row_of)

    @pl.when(six)
    def _():
        def row_of(q, base):
            extra = both(lambda m, n: fine_six(q, m, n), mean_of)
            if late:
                return lambda i, j: expand(even, base(i, j), extra(i, j))
            return both(lambda m, n: expand(even, base(2 * m, 2 * n), extra(2 * m, 2 * n)), mean_pair)

        each(row_of)

    @pl.when(jnp.logical_not(one | four | six))
    def _():
        def row_of(q, base):
            if late:
                return lambda i, j: expand(even, base(i, j))
            return both(lambda m, n: expand(even, base(2 * m, 2 * n)), mean_pair)

        each(row_of)


def inner_kernel(levels, sums, other, fine, out, held, sem):
    def write(g, q):
        return pltpu.make_async_copy(
            held.at[g, q], out.at[g, pl.ds(0, 7), :, q, pl.ds(0, 3)], sem.at[g, q]
        )

    for g in range(2):

        def put(q, i, j, pair):
            for h in range(2):
                held[g, q, i, h, j] = pair[h]

        def local_fine(q, m, n):
            return fine[g, m, n, q]

        emit(
            [(i, j) for i in range(7) for j in range(3)],
            False,
            levels,
            g,
            2,
            lambda q, m, n: sums[m, n, q] + other[m, n, q],
            local_fine,
            local_fine,
            local_fine,
            put,
            lambda q: write(g, q).start(),
        )
    for g in range(2):
        for q in range(8):
            write(g, q).wait()


def outer_kernel(
    levels, sums, other, fine, from_sy, from_sx, from_corner, fine_sy, _, out, last, side, sem
):
    def writes(g, q):
        return (
            pltpu.make_async_copy(last.at[g, q], out.at[g, 7, :, q], sem.at[0, g, q]),
            pltpu.make_async_copy(
                side.at[g, q], out.at[g, pl.ds(0, 7), :, q, 3], sem.at[1, g, q]
            ),
        )

    def nodal(q, m, n):
        if m < 4 and n < 2:
            return sums[m, n, q] + other[m, n, q]
        if m < 4:
            return from_sy[m, q]
        return from_sx[n, q] if n < 2 else from_corner[0, q]

    for g in range(2):

        def put(q, i, j, pair):
            for h in range(2):
                if i == 7:
                    last[g, q, h, j] = pair[h]
                else:
                    side[g, q, i, h] = pair[h]

        def done(q):
            for copy in writes(g, q):
                copy.start()

        def halo_sx(q, n):
            return from_sx[2 + 2 * g + n, q]

        def fine_one(q, m, n):
            value = fine[g, m, n, q] if n < 2 else fine_sy[g, m, q]
            if m == 3:
                value = value - 0.5 * (halo_sx(q, n) if n < 2 else from_corner[1 + g, q])
            return value

        def fine_four(q, m, n):
            value = fine[g, m, n, q] if m < 4 else halo_sx(q, n)
            if n == 1:
                value = value - 0.5 * (fine_sy[g, m, q] if m < 4 else from_corner[1 + g, q])
            return value

        def fine_six(q, m, n):
            if m < 4:
                return fine[g, m, n, q] if n < 2 else fine_sy[g, m, q]
            return halo_sx(q, n) if n < 2 else from_corner[1 + g, q]

        emit(
            [(7, j) for j in range(4)] + [(i, 3) for i in range(7)],
            True,
            levels,
            g,
            2,
            nodal,
            fine_one,
            fine_four,
            fine_six,
            put,
            done,
        )
    for g in range(2):
        for q in range(8):
            for copy in writes(g, q):
                copy.wait()


SCALARS = pl.BlockSpec(memory_space=pltpu.SMEM)
WHOLE = pl.BlockSpec(memory_space=pltpu.VMEM)
LEFT = pl.BlockSpec(memory_space=pl.ANY)
FAR = pl.BlockSpec(memory_space=pltpu.HBM)


def shape_of(*leading):
    return jax.ShapeDtypeStruct(leading + TILE, F32)


def held_in(*leading):
    return pltpu.VMEM(leading + TILE, F32)


def params(mebibytes=24):
    return pltpu.CompilerParams(vmem_limit_bytes=mebibytes * 1024 * 1024)


def cost(flops, size):
    return pl.CostEstimate(flops=flops, bytes_accessed=size, transcendentals=0)


def from_next(x, mesh_shape, step):
    sizes = [mesh_shape[axis] for axis in AXES]
    pairs = []
    for g in range(sizes[0]):
        for s in range(sizes[1]):
            for y in range(sizes[2]):
                source = [(c + d) % n for c, d, n in zip((g, s, y), step, sizes)]
                pairs.append(
                    (
                        (source[0] * sizes[1] + source[1]) * sizes[2] + source[2],
                        (g * sizes[1] + s) * sizes[2] + y,
                    )
                )
    return lax.ppermute(x, AXES, pairs)


def local_of(mesh_shape):
    def local(component_grids, levels, coefficients):
        u = component_grids.reshape((2, 4, 2, 2, 8, 2, 2) + TILE)
        sums, over_sy, coarse, odd = pl.pallas_call(
            first_kernel,
            out_shape=(
                shape_of(4, 2, 8),
                shape_of(2, 4, 8),
                shape_of(2, 2, 4, 2, 8),
                shape_of(2, 2, 4, 2, 8),
            ),
            in_specs=[FAR, FAR, FAR],
            out_specs=(WHOLE,) * 4,
            scratch_shapes=[
                pltpu.SMEM((2, 6), jnp.int32),
                pltpu.SMEM((2,), jnp.int32),
                pltpu.SemaphoreType.DMA((10,)),
            ],
            compiler_params=params(),
            cost_estimate=cost(1 << 20, 1 << 21),
            name="first",
        )(*[pltpu.with_memory_space_constraint(x, pltpu.HBM) for x in (levels, coefficients, u)])
        other = from_next(sums, mesh_shape, (1, 0, 0))
        fine_sy = from_next(over_sy, mesh_shape, (0, 0, 1))
        fine, over_sx, corner = pl.pallas_call(
            second_kernel,
            out_shape=(shape_of(2, 4, 2, 8), shape_of(2, 2, 8), shape_of(2, 8)),
            in_specs=[SCALARS, SCALARS, WHOLE, WHOLE],
            out_specs=(WHOLE, WHOLE, WHOLE),
            compiler_params=params(),
            cost_estimate=cost(1 << 20, 1 << 22),
            name="second",
        )(levels, coefficients, coarse, odd)
        to_sy, to_sx, to_corner = pl.pallas_call(
            third_kernel,
            out_shape=(shape_of(4, 8), shape_of(6, 8), shape_of(3, 8)),
            in_specs=[WHOLE] * 4,
            out_specs=(WHOLE,) * 3,
            compiler_params=params(),
            cost_estimate=cost(1 << 16, 1 << 20),
            name="third",
        )(sums, other, over_sx, corner)
        from_sy = from_next(to_sy, mesh_shape, (0, 0, 1))
        from_sx = from_next(to_sx, mesh_shape, (0, 1, 0))
        from_corner = from_next(to_corner, mesh_shape, (0, 1, 1))
        inner = pl.pallas_call(
            inner_kernel,
            out_shape=shape_of(2, 8, 2, 8, 4),
            in_specs=[SCALARS, WHOLE, WHOLE, WHOLE],
            out_specs=LEFT,
            scratch_shapes=[held_in(2, 8, 7, 2, 3), pltpu.SemaphoreType.DMA((2, 8))],
            compiler_params=params(),
            cost_estimate=cost(1 << 20, 1 << 22),
            name="inner",
        )(levels, sums, other, fine)
        out = pl.pallas_call(
            outer_kernel,
            out_shape=shape_of(2, 8, 2, 8, 4),
            in_specs=[SCALARS] + [WHOLE] * 7 + [LEFT],
            out_specs=LEFT,
            scratch_shapes=[
                held_in(2, 8, 2, 4),
                held_in(2, 8, 7, 2),
                pltpu.SemaphoreType.DMA((2, 2, 8)),
            ],
            input_output_aliases={8: 0},
            compiler_params=params(),
            cost_estimate=cost(1 << 20, 1 << 22),
            name="outer",
        )(levels, sums, other, fine, from_sy, from_sx, from_corner, fine_sy, inner)
        return out.reshape(component_grids.shape)

    return local


def solution(mesh):
    return jax.shard_map(
        local_of(dict(mesh.shape)),
        mesh=mesh,
        in_specs=(P("grp", "sx", None, None, "sy", None, None), P("grp", None), P("grp")),
        out_specs=P("grp", "sx", None, None, "sy", None, None),
        check_vma=False,
    )
```

```python
import jax
import jax.numpy as jnp
from jax import lax
from jax.experimental import pallas as pl
from jax.experimental.pallas import tpu as pltpu
from jax.sharding import PartitionSpec as P

AXES = ("grp", "sx", "sy")
FULL = (7, 4, 7)
REST = 5
VARYING = (0, 3, 5)
TILE = (8, 128)
F32 = jnp.float32


def even_lanes():
    return (lax.broadcasted_iota(jnp.int32, TILE, 1) & 1) == 0


def ahead(x, lanes=1):
    return pltpu.roll(x, 128 - lanes, 1)


def behind(x):
    return pltpu.roll(x, 1, 1)


def pack(even, a, b):
    return jnp.where(even, a, behind(b))


def pack_odd(even, a, b):
    return jnp.where(even, ahead(a), b)


def along_lanes(x):
    return x - 0.5 * (behind(x) + ahead(x))


def expand(even, p, odd=None):
    following = ahead(p)
    first, second = 0.5 * (behind(p) + following), 0.5 * (p + ahead(p, 2))
    if odd is not None:
        first, second = first + behind(odd), second + odd
    return jnp.where(even, p, first), jnp.where(even, following, second)


def mean_of(x, y):
    return 0.5 * (x + y)


def fine_in(levels, g, which):
    return levels[g, VARYING[which]] == FULL[which]


def weight_of(coefficients, g):
    return coefficients[g].astype(F32)


def first_kernel(
    far_levels, far_coefficients, u, edge, rest, over_sy, coarse, odd, levels, coefficients, sem
):
    scalars = [
        pltpu.make_async_copy(far_levels, levels, sem.at[0]),
        pltpu.make_async_copy(far_coefficients, coefficients, sem.at[1]),
    ]
    nodal = [
        pltpu.make_async_copy(u.at[g, :, 0, :, :, n, 0], coarse.at[g, n], sem.at[2 + 2 * g + n])
        for g in range(2)
        for n in range(2)
    ]
    for copy in scalars + nodal:
        copy.start()
    for copy in scalars:
        copy.wait()
    finer = []
    for g in range(2):
        one = fine_in(levels, g, 0).astype(jnp.int32)
        four = fine_in(levels, g, 1).astype(jnp.int32)
        for n in range(2):
            copy = pltpu.make_async_copy(
                u.at[g, :, one, :, :, n, four], odd.at[g, n], sem.at[6 + 2 * g + n]
            )
            copy.start()
            finer.append(copy)
    even = even_lanes()
    weights = [weight_of(coefficients, g) for g in range(2)]
    for copy in nodal:
        copy.wait()

    def add_up(q, m, n):
        a, b = (
            weights[0] * coarse[0, n, m, h, q] + weights[1] * coarse[1, n, m, h, q]
            for h in range(2)
        )
        return pack(even, a, b)

    @pl.loop(0, 4)
    def _(block):
        for k in range(2):
            q = 2 * block + k
            for m in range(4):
                edge[m, q] = add_up(q, m, 0)
            edge[4, q] = add_up(q, 0, 1)
            for m in range(3):
                rest[m, q] = add_up(q, m + 1, 1)
            for m in range(3, REST):
                rest[m, q] = edge[4, q]

    for copy in finer:
        copy.wait()
    for g in range(2):
        one, six = fine_in(levels, g, 0), fine_in(levels, g, 2)

        @pl.when(one)
        def _():
            for m in range(4):
                for q in range(8):
                    halves = []
                    for h in range(2):
                        parents = coarse[g, 0, m, h, q]
                        if m < 3:
                            parents = parents + coarse[g, 0, m + 1, h, q]
                        halves.append(weights[g] * (odd[g, 0, m, h, q] - 0.5 * parents))
                    over_sy[g, m, q] = pack(even, *halves)

        @pl.when(six)
        def _():
            for m in range(4):
                for q in range(8):
                    halves = [weights[g] * along_lanes(coarse[g, 0, m, h, q]) for h in range(2)]
                    over_sy[g, m, q] = pack_odd(even, *halves)

        @pl.when(jnp.logical_not(one | six))
        def _():
            for m in range(4):
                for q in range(8):
                    halves = [weights[g] * coarse[g, 0, m, h, q] for h in range(2)]
                    over_sy[g, m, q] = pack(even, *halves)


def second_kernel(levels, coefficients, coarse, odd, fine, over_sx, corner):
    even = even_lanes()
    for g in range(2):
        weight = weight_of(coefficients, g)
        one, four, six = (fine_in(levels, g, which) for which in range(3))

        def nodal(n, m, q):
            return pack(even, *[weight * coarse[g, n, m, h, q] for h in range(2)])

        def each(body):
            @pl.loop(0, 4)
            def _(block):
                for k in range(2):
                    body(2 * block + k)

        @pl.when(one)
        def _():
            def body(q):
                for n in range(2):
                    for m in range(4):
                        halves = []
                        for h in range(2):
                            parents = coarse[g, n, m, h, q]
                            if m < 3:
                                parents = parents + coarse[g, n, m + 1, h, q]
                            halves.append(weight * (odd[g, n, m, h, q] - 0.5 * parents))
                        fine[g, m, n, q] = pack(even, *halves)
                    edge = nodal(n, 0, q)
                    over_sx[g, n, q] = edge
                    if n == 0:
                        corner[g, q] = edge

            each(body)

        @pl.when(four)
        def _():
            def body(q):
                for n in range(2):
                    for m in range(4):
                        halves = []
                        for h in range(2):
                            parents = coarse[g, n, m, h, q]
                            if n < 1:
                                parents = parents + coarse[g, n + 1, m, h, q]
                            halves.append(weight * (odd[g, n, m, h, q] - 0.5 * parents))
                        packed = pack(even, *halves)
                        fine[g, m, n, q] = packed
                        if m == 0:
                            over_sx[g, n, q] = packed
                corner[g, q] = nodal(0, 0, q)

            each(body)

        @pl.when(six)
        def _():
            def body(q):
                for n in range(2):
                    for m in range(4):
                        halves = [weight * along_lanes(coarse[g, n, m, h, q]) for h in range(2)]
                        packed = pack_odd(even, *halves)
                        fine[g, m, n, q] = packed
                        if m == 0:
                            over_sx[g, n, q] = packed
                            if n == 0:
                                corner[g, q] = packed

            each(body)

        @pl.when(jnp.logical_not(one | four | six))
        def _():
            over_sx[g] = jnp.zeros(over_sx.shape[1:], F32)
            corner[g] = jnp.zeros(corner.shape[1:], F32)


def third_kernel(edge, other_edge, corner, to_sy, to_sx, to_corner):
    for m in range(4):
        to_sy[m] = edge[m] + other_edge[m]
    to_sx[0] = to_sy[0]
    to_sx[1] = edge[4] + other_edge[4]
    to_corner[0] = to_sy[0]
    for g in range(2):
        to_corner[1 + g] = corner[g]


def total(edge, other_edge, rest, other_rest):
    def nodal(q, m, n):
        if n == 0 or m == 0:
            place = m if n == 0 else 4
            return edge[place, q] + other_edge[place, q]
        return rest[m - 1, q] + other_rest[m - 1, q]

    return nodal


def remembered(rule):
    seen = {}

    def value(i, j):
        if (i, j) not in seen:
            seen[i, j] = rule(value, i, j)
        return seen[i, j]

    return value


def mean_pair(x, y):
    return tuple(mean_of(a, b) for a, b in zip(x, y))


def along_one(value, i, j):
    return value(i - 1, j), value(i + 1, j)


def along_four(value, i, j):
    return value(i, j - 1), value(i, j + 1)


def emit(points, late, levels, g, columns, nodal, fine_one, fine_four, fine_six, put, done):
    even = even_lanes()
    one, four, six = (fine_in(levels, g, which) for which in range(3))

    def both(leaf, mean):
        def rule(value, i, j):
            if i % 2:
                return mean(*along_one(value, i, j))
            if j % 2:
                return mean(*along_four(value, i, j))
            return leaf(i // 2, j // 2)

        return remembered(rule)

    def each(row_of):
        @pl.loop(0, 8 // columns)
        def _(block):
            for k in range(columns):
                q = block * columns + k
                row = row_of(q, both(lambda m, n: nodal(q, m, n), mean_of))
                for i, j in points:
                    put(q, i, j, row(i, j))
                done(q)

    @pl.when(one)
    def _():
        def row_of(q, base):
            def extra(value, i, j):
                if j % 2:
                    return mean_of(*along_four(value, i, j))
                return fine_one(q, i // 2, j // 2)

            extra = remembered(extra)

            def rule(value, i, j):
                if j % 2 and not late:
                    return mean_pair(*along_four(value, i, j))
                return expand(even, base(i, j) + extra(i, j) if i % 2 else base(i, j))

            return remembered(rule)

        each(row_of)

    @pl.when(four)
    def _():
        def row_of(q, base):
            def extra(value, i, j):
                if i % 2:
                    return mean_of(*along_one(value, i, j))
                return fine_four(q, i // 2, j // 2)

            extra = remembered(extra)

            def rule(value, i, j):
                if i % 2 and not late:
                    return mean_pair(*along_one(value, i, j))
                return expand(even, base(i, j) + extra(i, j) if j % 2 else base(i, j))

            return remembered(rule)

        each(row_of)

    @pl.when(six)
    def _():
        def row_of(q, base):
            extra = both(lambda m, n: fine_six(q, m, n), mean_of)
            if late:
                return lambda i, j: expand(even, base(i, j), extra(i, j))
            return both(lambda m, n: expand(even, base(2 * m, 2 * n), extra(2 * m, 2 * n)), mean_pair)

        each(row_of)

    @pl.when(jnp.logical_not(one | four | six))
    def _():
        def row_of(q, base):
            if late:
                return lambda i, j: expand(even, base(i, j))
            return both(lambda m, n: expand(even, base(2 * m, 2 * n)), mean_pair)

        each(row_of)


def inner_kernel(levels, edge, other_edge, rest, other_rest, fine, out, held, sem):
    def write(g, q):
        return pltpu.make_async_copy(
            held.at[g, q], out.at[g, pl.ds(0, 7), :, q, pl.ds(0, 3)], sem.at[g, q]
        )

    for g in range(2):

        def put(q, i, j, pair):
            for h in range(2):
                held[g, q, i, h, j] = pair[h]

        def local_fine(q, m, n):
            return fine[g, m, n, q]

        emit(
            [(i, j) for i in range(7) for j in range(3)],
            False,
            levels,
            g,
            4,
            total(edge, other_edge, rest, other_rest),
            local_fine,
            local_fine,
            local_fine,
            put,
            lambda q: write(g, q).start(),
        )
    for g in range(2):
        for q in range(8):
            write(g, q).wait()


def outer_kernel(
    levels,
    edge,
    other_edge,
    rest,
    other_rest,
    fine,
    from_sy,
    from_sx,
    from_corner,
    from_ex,
    fine_sy,
    _,
    out,
    last,
    side,
    sem,
):
    local = total(edge, other_edge, rest, other_rest)

    def writes(g, q):
        return (
            pltpu.make_async_copy(last.at[g, q], out.at[g, 7, :, q], sem.at[0, g, q]),
            pltpu.make_async_copy(
                side.at[g, q], out.at[g, pl.ds(0, 7), :, q, 3], sem.at[1, g, q]
            ),
        )

    def nodal(q, m, n):
        if m < 4 and n < 2:
            return local(q, m, n)
        if m < 4:
            return from_sy[m, q]
        return from_sx[n, q] if n < 2 else from_corner[0, q]

    for g in range(2):

        def put(q, i, j, pair):
            for h in range(2):
                if i == 7:
                    last[g, q, h, j] = pair[h]
                else:
                    side[g, q, i, h] = pair[h]

        def done(q):
            for copy in writes(g, q):
                copy.start()

        def halo_sx(q, n):
            return from_ex[g, n, q]

        def fine_one(q, m, n):
            value = fine[g, m, n, q] if n < 2 else fine_sy[g, m, q]
            if m == 3:
                value = value - 0.5 * (halo_sx(q, n) if n < 2 else from_corner[1 + g, q])
            return value

        def fine_four(q, m, n):
            value = fine[g, m, n, q] if m < 4 else halo_sx(q, n)
            if n == 1:
                value = value - 0.5 * (fine_sy[g, m, q] if m < 4 else from_corner[1 + g, q])
            return value

        def fine_six(q, m, n):
            if m < 4:
                return fine[g, m, n, q] if n < 2 else fine_sy[g, m, q]
            return halo_sx(q, n) if n < 2 else from_corner[1 + g, q]

        emit(
            [(7, j) for j in range(4)] + [(i, 3) for i in range(7)],
            True,
            levels,
            g,
            8,
            nodal,
            fine_one,
            fine_four,
            fine_six,
            put,
            done,
        )
    for g in range(2):
        for q in range(8):
            for copy in writes(g, q):
                copy.wait()


SCALARS = pl.BlockSpec(memory_space=pltpu.SMEM)
WHOLE = pl.BlockSpec(memory_space=pltpu.VMEM)
LEFT = pl.BlockSpec(memory_space=pl.ANY)
FAR = pl.BlockSpec(memory_space=pltpu.HBM)


def shape_of(*leading):
    return jax.ShapeDtypeStruct(leading + TILE, F32)


def held_in(*leading):
    return pltpu.VMEM(leading + TILE, F32)


def params(mebibytes=24):
    return pltpu.CompilerParams(vmem_limit_bytes=mebibytes * 1024 * 1024)


def cost(flops, size):
    return pl.CostEstimate(flops=flops, bytes_accessed=size, transcendentals=0)


def from_next(x, mesh_shape, step, cross=False):
    sizes = [mesh_shape[axis] for axis in AXES]
    pairs = []
    for g in range(sizes[0]):
        for s in range(sizes[1]):
            for y in range(sizes[2]):
                turn = s % 2 if cross else 0
                source = [(c + d) % n for c, d, n in zip((g + turn, s, y), step, sizes)]
                pairs.append(
                    (
                        (source[0] * sizes[1] + source[1]) * sizes[2] + source[2],
                        (g * sizes[1] + s) * sizes[2] + y,
                    )
                )
    return lax.ppermute(x, AXES, pairs)


def local_of(mesh_shape):
    def local(component_grids, levels, coefficients):
        u = component_grids.reshape((2, 4, 2, 2, 8, 2, 2) + TILE)
        edge, rest, over_sy, coarse, odd = pl.pallas_call(
            first_kernel,
            out_shape=(
                shape_of(5, 8),
                shape_of(REST, 8),
                shape_of(2, 4, 8),
                shape_of(2, 2, 4, 2, 8),
                shape_of(2, 2, 4, 2, 8),
            ),
            in_specs=[FAR, FAR, FAR],
            out_specs=(WHOLE,) * 5,
            scratch_shapes=[
                pltpu.SMEM((2, 6), jnp.int32),
                pltpu.SMEM((2,), jnp.int32),
                pltpu.SemaphoreType.DMA((10,)),
            ],
            compiler_params=params(),
            cost_estimate=cost(1 << 20, 1 << 21),
            name="first",
        )(*[pltpu.with_memory_space_constraint(x, pltpu.HBM) for x in (levels, coefficients, u)])
        other_edge = from_next(edge, mesh_shape, (1, 0, 0))
        other_rest = from_next(rest, mesh_shape, (1, 0, 0))
        fine_sy = from_next(over_sy, mesh_shape, (0, 0, 1))
        fine, over_sx, corner = pl.pallas_call(
            second_kernel,
            out_shape=(shape_of(2, 4, 2, 8), shape_of(2, 2, 8), shape_of(2, 8)),
            in_specs=[SCALARS, SCALARS, WHOLE, WHOLE],
            out_specs=(WHOLE, WHOLE, WHOLE),
            compiler_params=params(),
            cost_estimate=cost(1 << 20, 1 << 22),
            name="second",
        )(levels, coefficients, coarse, odd)
        to_sy, to_sx, to_corner = pl.pallas_call(
            third_kernel,
            out_shape=(shape_of(4, 8), shape_of(2, 8), shape_of(3, 8)),
            in_specs=[WHOLE] * 3,
            out_specs=(WHOLE,) * 3,
            compiler_params=params(),
            cost_estimate=cost(1 << 16, 1 << 20),
            name="third",
        )(edge, other_edge, corner)
        from_sy = from_next(to_sy, mesh_shape, (0, 0, 1))
        from_ex = from_next(over_sx, mesh_shape, (0, 1, 0))
        from_sx = from_next(to_sx, mesh_shape, (0, 1, 0), cross=True)
        from_corner = from_next(to_corner, mesh_shape, (0, 1, 1))
        parts = (edge, other_edge, rest, other_rest)
        inner = pl.pallas_call(
            inner_kernel,
            out_shape=shape_of(2, 8, 2, 8, 4),
            in_specs=[SCALARS] + [WHOLE] * 5,
            out_specs=LEFT,
            scratch_shapes=[held_in(2, 8, 7, 2, 3), pltpu.SemaphoreType.DMA((2, 8))],
            compiler_params=params(),
            cost_estimate=cost(1 << 20, 1 << 22),
            name="inner",
        )(levels, *parts, fine)
        out = pl.pallas_call(
            outer_kernel,
            out_shape=shape_of(2, 8, 2, 8, 4),
            in_specs=[SCALARS] + [WHOLE] * 10 + [LEFT],
            out_specs=LEFT,
            scratch_shapes=[
                held_in(2, 8, 2, 4),
                held_in(2, 8, 7, 2),
                pltpu.SemaphoreType.DMA((2, 2, 8)),
            ],
            input_output_aliases={11: 0},
            compiler_params=params(),
            cost_estimate=cost(1 << 20, 1 << 22),
            name="outer",
        )(levels, *parts, fine, from_sy, from_sx, from_corner, from_ex, fine_sy, inner)
        return out.reshape(component_grids.shape)

    return local


def solution(mesh):
    return jax.shard_map(
        local_of(dict(mesh.shape)),
        mesh=mesh,
        in_specs=(P("grp", "sx", None, None, "sy", None, None), P("grp", None), P("grp")),
        out_specs=P("grp", "sx", None, None, "sy", None, None),
        check_vma=False,
    )
```

```python
import jax
import jax.numpy as jnp
from jax import lax
from jax.experimental import pallas as pl
from jax.experimental.pallas import tpu as pltpu
from jax.sharding import PartitionSpec as P

AXES = ("grp", "sx", "sy")
FULL = (7, 4, 7)
VARYING = (0, 3, 5)
TILE = (8, 128)
F32 = jnp.float32


def even_lanes():
    return (lax.broadcasted_iota(jnp.int32, TILE, 1) & 1) == 0


def ahead(x, lanes=1):
    return pltpu.roll(x, 128 - lanes, 1)


def behind(x):
    return pltpu.roll(x, 1, 1)


def pack(even, a, b):
    return jnp.where(even, a, behind(b))


def pack_odd(even, a, b):
    return jnp.where(even, ahead(a), b)


def along_lanes(x):
    return x - 0.5 * (behind(x) + ahead(x))


def expand(even, p, odd=None):
    following = ahead(p)
    first, second = 0.5 * (behind(p) + following), 0.5 * (p + ahead(p, 2))
    if odd is not None:
        first, second = first + behind(odd), second + odd
    return jnp.where(even, p, first), jnp.where(even, following, second)


def mean_of(x, y):
    return 0.5 * (x + y)


def fine_in(levels, g, which):
    return levels[g, VARYING[which]] == FULL[which]


def weight_of(coefficients, g):
    return coefficients[g].astype(F32)


def added(even, weights, coarse, q, m, n):
    a, b = (
        weights[0] * coarse[0, n, m, h, q] + weights[1] * coarse[1, n, m, h, q] for h in range(2)
    )
    return pack(even, a, b)


def first_kernel(
    far_levels, far_coefficients, u, edge, over_sy, coarse, odd, levels, coefficients, sem
):
    scalars = [
        pltpu.make_async_copy(far_levels, levels, sem.at[0]),
        pltpu.make_async_copy(far_coefficients, coefficients, sem.at[1]),
    ]
    nodal = [
        pltpu.make_async_copy(u.at[g, :, 0, :, :, n, 0], coarse.at[g, n], sem.at[2 + 2 * g + n])
        for g in range(2)
        for n in range(2)
    ]
    for copy in scalars + nodal:
        copy.start()
    for copy in scalars:
        copy.wait()
    finer = []
    for g in range(2):
        one = fine_in(levels, g, 0).astype(jnp.int32)
        four = fine_in(levels, g, 1).astype(jnp.int32)
        for n in range(2):
            copy = pltpu.make_async_copy(
                u.at[g, :, one, :, :, n, four], odd.at[g, n], sem.at[6 + 2 * g + n]
            )
            copy.start()
            finer.append(copy)
    even = even_lanes()
    weights = [weight_of(coefficients, g) for g in range(2)]
    for copy in nodal:
        copy.wait()

    @pl.loop(0, 4)
    def _(block):
        for k in range(2):
            q = 2 * block + k
            for m in range(4):
                edge[m, q] = added(even, weights, coarse, q, m, 0)
            edge[4, q] = added(even, weights, coarse, q, 0, 1)

    for copy in finer:
        copy.wait()
    for g in range(2):
        one, six = fine_in(levels, g, 0), fine_in(levels, g, 2)

        @pl.when(one)
        def _():
            for m in range(4):
                for q in range(8):
                    halves = []
                    for h in range(2):
                        parents = coarse[g, 0, m, h, q]
                        if m < 3:
                            parents = parents + coarse[g, 0, m + 1, h, q]
                        halves.append(weights[g] * (odd[g, 0, m, h, q] - 0.5 * parents))
                    over_sy[g, m, q] = pack(even, *halves)

        @pl.when(six)
        def _():
            for m in range(4):
                for q in range(8):
                    halves = [weights[g] * along_lanes(coarse[g, 0, m, h, q]) for h in range(2)]
                    over_sy[g, m, q] = pack_odd(even, *halves)

        @pl.when(jnp.logical_not(one | six))
        def _():
            for m in range(4):
                for q in range(8):
                    halves = [weights[g] * coarse[g, 0, m, h, q] for h in range(2)]
                    over_sy[g, m, q] = pack(even, *halves)


def second_kernel(levels, coefficients, coarse, odd, fine, over_sx, corner, rest):
    even = even_lanes()
    weights = [weight_of(coefficients, g) for g in range(2)]

    @pl.loop(0, 4)
    def _(block):
        for k in range(2):
            q = 2 * block + k
            for m in range(3):
                rest[m, q] = added(even, weights, coarse, q, m + 1, 1)

    for g in range(2):
        weight = weight_of(coefficients, g)
        one, four, six = (fine_in(levels, g, which) for which in range(3))

        def nodal(n, m, q):
            return pack(even, *[weight * coarse[g, n, m, h, q] for h in range(2)])

        def each(body):
            @pl.loop(0, 4)
            def _(block):
                for k in range(2):
                    body(2 * block + k)

        @pl.when(one)
        def _():
            def body(q):
                for n in range(2):
                    for m in range(4):
                        halves = []
                        for h in range(2):
                            parents = coarse[g, n, m, h, q]
                            if m < 3:
                                parents = parents + coarse[g, n, m + 1, h, q]
                            halves.append(weight * (odd[g, n, m, h, q] - 0.5 * parents))
                        fine[g, m, n, q] = pack(even, *halves)
                    edge = nodal(n, 0, q)
                    over_sx[g, n, q] = edge
                    if n == 0:
                        corner[g, q] = edge

            each(body)

        @pl.when(four)
        def _():
            def body(q):
                for n in range(2):
                    for m in range(4):
                        halves = []
                        for h in range(2):
                            parents = coarse[g, n, m, h, q]
                            if n < 1:
                                parents = parents + coarse[g, n + 1, m, h, q]
                            halves.append(weight * (odd[g, n, m, h, q] - 0.5 * parents))
                        packed = pack(even, *halves)
                        fine[g, m, n, q] = packed
                        if m == 0:
                            over_sx[g, n, q] = packed
                corner[g, q] = nodal(0, 0, q)

            each(body)

        @pl.when(six)
        def _():
            def body(q):
                for n in range(2):
                    for m in range(4):
                        halves = [weight * along_lanes(coarse[g, n, m, h, q]) for h in range(2)]
                        packed = pack_odd(even, *halves)
                        fine[g, m, n, q] = packed
                        if m == 0:
                            over_sx[g, n, q] = packed
                            if n == 0:
                                corner[g, q] = packed

            each(body)

        @pl.when(jnp.logical_not(one | four | six))
        def _():
            over_sx[g] = jnp.zeros(over_sx.shape[1:], F32)
            corner[g] = jnp.zeros(corner.shape[1:], F32)


def third_kernel(edge, other_edge, corner, to_sy, to_sx, to_corner):
    for m in range(4):
        to_sy[m] = edge[m] + other_edge[m]
    to_sx[0] = to_sy[0]
    to_sx[1] = edge[4] + other_edge[4]
    to_corner[0] = to_sy[0]
    for g in range(2):
        to_corner[1 + g] = corner[g]


def total(edge, other_edge, rest, other_rest):
    def nodal(q, m, n):
        if n == 0 or m == 0:
            place = m if n == 0 else 4
            return edge[place, q] + other_edge[place, q]
        return rest[m - 1, q] + other_rest[m - 1, q]

    return nodal


def remembered(rule):
    seen = {}

    def value(i, j):
        if (i, j) not in seen:
            seen[i, j] = rule(value, i, j)
        return seen[i, j]

    return value


def mean_pair(x, y):
    return tuple(mean_of(a, b) for a, b in zip(x, y))


def along_one(value, i, j):
    return value(i - 1, j), value(i + 1, j)


def along_four(value, i, j):
    return value(i, j - 1), value(i, j + 1)


def emit(points, late, levels, g, columns, nodal, fine_one, fine_four, fine_six, put, done):
    even = even_lanes()
    one, four, six = (fine_in(levels, g, which) for which in range(3))

    def both(leaf, mean):
        def rule(value, i, j):
            if i % 2:
                return mean(*along_one(value, i, j))
            if j % 2:
                return mean(*along_four(value, i, j))
            return leaf(i // 2, j // 2)

        return remembered(rule)

    def each(row_of):
        @pl.loop(0, 8 // columns)
        def _(block):
            for k in range(columns):
                q = block * columns + k
                row = row_of(q, both(lambda m, n: nodal(q, m, n), mean_of))
                for i, j in points:
                    put(q, i, j, row(i, j))
                done(q)

    @pl.when(one)
    def _():
        def row_of(q, base):
            def extra(value, i, j):
                if j % 2:
                    return mean_of(*along_four(value, i, j))
                return fine_one(q, i // 2, j // 2)

            extra = remembered(extra)

            def rule(value, i, j):
                if j % 2 and not late:
                    return mean_pair(*along_four(value, i, j))
                return expand(even, base(i, j) + extra(i, j) if i % 2 else base(i, j))

            return remembered(rule)

        each(row_of)

    @pl.when(four)
    def _():
        def row_of(q, base):
            def extra(value, i, j):
                if i % 2:
                    return mean_of(*along_one(value, i, j))
                return fine_four(q, i // 2, j // 2)

            extra = remembered(extra)

            def rule(value, i, j):
                if i % 2 and not late:
                    return mean_pair(*along_one(value, i, j))
                return expand(even, base(i, j) + extra(i, j) if j % 2 else base(i, j))

            return remembered(rule)

        each(row_of)

    @pl.when(six)
    def _():
        def row_of(q, base):
            extra = both(lambda m, n: fine_six(q, m, n), mean_of)
            if late:
                return lambda i, j: expand(even, base(i, j), extra(i, j))
            return both(lambda m, n: expand(even, base(2 * m, 2 * n), extra(2 * m, 2 * n)), mean_pair)

        each(row_of)

    @pl.when(jnp.logical_not(one | four | six))
    def _():
        def row_of(q, base):
            if late:
                return lambda i, j: expand(even, base(i, j))
            return both(lambda m, n: expand(even, base(2 * m, 2 * n)), mean_pair)

        each(row_of)


def inner_kernel(levels, edge, other_edge, rest, other_rest, fine, out, held, sem):
    def write(g, q):
        return pltpu.make_async_copy(
            held.at[g, q], out.at[g, pl.ds(0, 7), :, q, pl.ds(0, 3)], sem.at[g, q]
        )

    for g in range(2):

        def put(q, i, j, pair):
            for h in range(2):
                held[g, q, i, h, j] = pair[h]

        def local_fine(q, m, n):
            return fine[g, m, n, q]

        emit(
            [(i, j) for i in range(7) for j in range(3)],
            False,
            levels,
            g,
            4,
            total(edge, other_edge, rest, other_rest),
            local_fine,
            local_fine,
            local_fine,
            put,
            lambda q: write(g, q).start(),
        )
    for g in range(2):
        for q in range(8):
            write(g, q).wait()


def outer_kernel(
    levels,
    edge,
    other_edge,
    rest,
    other_rest,
    fine,
    from_sy,
    from_sx,
    from_corner,
    from_ex,
    fine_sy,
    _,
    out,
    last,
    side,
    sem,
):
    local = total(edge, other_edge, rest, other_rest)

    def writes(g, q):
        return (
            pltpu.make_async_copy(last.at[g, q], out.at[g, 7, :, q], sem.at[0, g, q]),
            pltpu.make_async_copy(
                side.at[g, q], out.at[g, pl.ds(0, 7), :, q, 3], sem.at[1, g, q]
            ),
        )

    def nodal(q, m, n):
        if m < 4 and n < 2:
            return local(q, m, n)
        if m < 4:
            return from_sy[m, q]
        return from_sx[n, q] if n < 2 else from_corner[0, q]

    for g in range(2):

        def put(q, i, j, pair):
            for h in range(2):
                if i == 7:
                    last[g, q, h, j] = pair[h]
                else:
                    side[g, q, i, h] = pair[h]

        def done(q):
            for copy in writes(g, q):
                copy.start()

        def halo_sx(q, n):
            return from_ex[g, n, q]

        def fine_one(q, m, n):
            value = fine[g, m, n, q] if n < 2 else fine_sy[g, m, q]
            if m == 3:
                value = value - 0.5 * (halo_sx(q, n) if n < 2 else from_corner[1 + g, q])
            return value

        def fine_four(q, m, n):
            value = fine[g, m, n, q] if m < 4 else halo_sx(q, n)
            if n == 1:
                value = value - 0.5 * (fine_sy[g, m, q] if m < 4 else from_corner[1 + g, q])
            return value

        def fine_six(q, m, n):
            if m < 4:
                return fine[g, m, n, q] if n < 2 else fine_sy[g, m, q]
            return halo_sx(q, n) if n < 2 else from_corner[1 + g, q]

        emit(
            [(7, j) for j in range(4)] + [(i, 3) for i in range(7)],
            True,
            levels,
            g,
            8,
            nodal,
            fine_one,
            fine_four,
            fine_six,
            put,
            done,
        )
    for g in range(2):
        for q in range(8):
            for copy in writes(g, q):
                copy.wait()


SCALARS = pl.BlockSpec(memory_space=pltpu.SMEM)
WHOLE = pl.BlockSpec(memory_space=pltpu.VMEM)
LEFT = pl.BlockSpec(memory_space=pl.ANY)
FAR = pl.BlockSpec(memory_space=pltpu.HBM)


def shape_of(*leading):
    return jax.ShapeDtypeStruct(leading + TILE, F32)


def held_in(*leading):
    return pltpu.VMEM(leading + TILE, F32)


def params(mebibytes=24):
    return pltpu.CompilerParams(vmem_limit_bytes=mebibytes * 1024 * 1024)


def cost(flops, size):
    return pl.CostEstimate(flops=flops, bytes_accessed=size, transcendentals=0)


def from_next(x, mesh_shape, step, cross=False):
    sizes = [mesh_shape[axis] for axis in AXES]
    pairs = []
    for g in range(sizes[0]):
        for s in range(sizes[1]):
            for y in range(sizes[2]):
                turn = s % 2 if cross else 0
                source = [(c + d) % n for c, d, n in zip((g + turn, s, y), step, sizes)]
                pairs.append(
                    (
                        (source[0] * sizes[1] + source[1]) * sizes[2] + source[2],
                        (g * sizes[1] + s) * sizes[2] + y,
                    )
                )
    return lax.ppermute(x, AXES, pairs)


def local_of(mesh_shape):
    def local(component_grids, levels, coefficients):
        u = component_grids.reshape((2, 4, 2, 2, 8, 2, 2) + TILE)
        edge, over_sy, coarse, odd = pl.pallas_call(
            first_kernel,
            out_shape=(
                shape_of(5, 8),
                shape_of(2, 4, 8),
                shape_of(2, 2, 4, 2, 8),
                shape_of(2, 2, 4, 2, 8),
            ),
            in_specs=[FAR, FAR, FAR],
            out_specs=(WHOLE,) * 4,
            scratch_shapes=[
                pltpu.SMEM((2, 6), jnp.int32),
                pltpu.SMEM((2,), jnp.int32),
                pltpu.SemaphoreType.DMA((10,)),
            ],
            compiler_params=params(),
            cost_estimate=cost(1 << 20, 1 << 21),
            name="first",
        )(*[pltpu.with_memory_space_constraint(x, pltpu.HBM) for x in (levels, coefficients, u)])
        other_edge = from_next(edge, mesh_shape, (1, 0, 0))
        fine_sy = from_next(over_sy, mesh_shape, (0, 0, 1))
        fine, over_sx, corner, rest = pl.pallas_call(
            second_kernel,
            out_shape=(shape_of(2, 4, 2, 8), shape_of(2, 2, 8), shape_of(2, 8), shape_of(3, 8)),
            in_specs=[SCALARS, SCALARS, WHOLE, WHOLE],
            out_specs=(WHOLE,) * 4,
            compiler_params=params(),
            cost_estimate=cost(1 << 20, 1 << 22),
            name="second",
        )(levels, coefficients, coarse, odd)
        other_rest = from_next(rest, mesh_shape, (1, 0, 0))
        to_sy, to_sx, to_corner = pl.pallas_call(
            third_kernel,
            out_shape=(shape_of(4, 8), shape_of(2, 8), shape_of(3, 8)),
            in_specs=[WHOLE] * 3,
            out_specs=(WHOLE,) * 3,
            compiler_params=params(),
            cost_estimate=cost(1 << 16, 1 << 20),
            name="third",
        )(edge, other_edge, corner)
        from_sy = from_next(to_sy, mesh_shape, (0, 0, 1))
        from_ex = from_next(over_sx, mesh_shape, (0, 1, 0))
        from_sx = from_next(to_sx, mesh_shape, (0, 1, 0), cross=True)
        from_corner = from_next(to_corner, mesh_shape, (0, 1, 1))
        parts = (edge, other_edge, rest, other_rest)
        inner = pl.pallas_call(
            inner_kernel,
            out_shape=shape_of(2, 8, 2, 8, 4),
            in_specs=[SCALARS] + [WHOLE] * 5,
            out_specs=LEFT,
            scratch_shapes=[held_in(2, 8, 7, 2, 3), pltpu.SemaphoreType.DMA((2, 8))],
            compiler_params=params(),
            cost_estimate=cost(1 << 20, 1 << 22),
            name="inner",
        )(levels, *parts, fine)
        out = pl.pallas_call(
            outer_kernel,
            out_shape=shape_of(2, 8, 2, 8, 4),
            in_specs=[SCALARS] + [WHOLE] * 10 + [LEFT],
            out_specs=LEFT,
            scratch_shapes=[
                held_in(2, 8, 2, 4),
                held_in(2, 8, 7, 2),
                pltpu.SemaphoreType.DMA((2, 2, 8)),
            ],
            input_output_aliases={11: 0},
            compiler_params=params(),
            cost_estimate=cost(1 << 20, 1 << 22),
            name="outer",
        )(levels, *parts, fine, from_sy, from_sx, from_corner, from_ex, fine_sy, inner)
        return out.reshape(component_grids.shape)

    return local


def solution(mesh):
    return jax.shard_map(
        local_of(dict(mesh.shape)),
        mesh=mesh,
        in_specs=(P("grp", "sx", None, None, "sy", None, None), P("grp", None), P("grp")),
        out_specs=P("grp", "sx", None, None, "sy", None, None),
        check_vma=False,
    )
```

```python
import jax
import jax.numpy as jnp
from jax import lax
from jax.experimental import pallas as pl
from jax.experimental.pallas import tpu as pltpu
from jax.sharding import PartitionSpec as P

AXES = ("grp", "sx", "sy")
FULL = (7, 4, 7)
VARYING = (0, 3, 5)
TILE = (8, 128)
F32 = jnp.float32


def even_lanes():
    return (lax.broadcasted_iota(jnp.int32, TILE, 1) & 1) == 0


def ahead(x, lanes=1):
    return pltpu.roll(x, 128 - lanes, 1)


def behind(x):
    return pltpu.roll(x, 1, 1)


def pack(even, a, b):
    return jnp.where(even, a, behind(b))


def pack_odd(even, a, b):
    return jnp.where(even, ahead(a), b)


def along_lanes(x):
    return x - 0.5 * (behind(x) + ahead(x))


def expand(even, p, odd=None):
    following = ahead(p)
    first, second = 0.5 * (behind(p) + following), 0.5 * (p + ahead(p, 2))
    if odd is not None:
        first, second = first + behind(odd), second + odd
    return jnp.where(even, p, first), jnp.where(even, following, second)


def mean_of(x, y):
    return 0.5 * (x + y)


def fine_in(levels, g, which):
    return levels[g, VARYING[which]] == FULL[which]


def weight_of(coefficients, g):
    return coefficients[g].astype(F32)


def added(even, weights, coarse, q, m, n):
    a, b = (
        weights[0] * coarse[0, n, m, h, q] + weights[1] * coarse[1, n, m, h, q] for h in range(2)
    )
    return pack(even, a, b)


def first_kernel(
    far_levels, far_coefficients, u, edge, over_sy, coarse, odd, levels, coefficients, sem
):
    scalars = [
        pltpu.make_async_copy(far_levels, levels, sem.at[0]),
        pltpu.make_async_copy(far_coefficients, coefficients, sem.at[1]),
    ]
    nodal = [
        pltpu.make_async_copy(u.at[g, :, 0, :, :, n, 0], coarse.at[g, n], sem.at[2 + 2 * g + n])
        for g in range(2)
        for n in range(2)
    ]
    finer = [
        pltpu.make_async_copy(
            u.at[g, :, one, :, :, n, 1 - one], odd.at[1 - one, g, n], sem.at[2 + 4 * (2 - one) + 2 * g + n]
        )
        for one in (1, 0)
        for g in range(2)
        for n in range(2)
    ]
    for copy in scalars + nodal + finer:
        copy.start()
    for copy in scalars:
        copy.wait()
    even = even_lanes()
    weights = [weight_of(coefficients, g) for g in range(2)]
    for copy in nodal:
        copy.wait()

    @pl.loop(0, 2)
    def _(block):
        for k in range(4):
            q = 4 * block + k
            for m in range(4):
                edge[m, q] = added(even, weights, coarse, q, m, 0)
            edge[4, q] = added(even, weights, coarse, q, 0, 1)

    for copy in finer:
        copy.wait()
    for g in range(2):
        one, six = fine_in(levels, g, 0), fine_in(levels, g, 2)

        @pl.when(one)
        def _():
            for m in range(4):
                for q in range(8):
                    halves = []
                    for h in range(2):
                        parents = coarse[g, 0, m, h, q]
                        if m < 3:
                            parents = parents + coarse[g, 0, m + 1, h, q]
                        halves.append(weights[g] * (odd[0, g, 0, m, h, q] - 0.5 * parents))
                    over_sy[g, m, q] = pack(even, *halves)

        @pl.when(six)
        def _():
            for m in range(4):
                for q in range(8):
                    halves = [weights[g] * along_lanes(coarse[g, 0, m, h, q]) for h in range(2)]
                    over_sy[g, m, q] = pack_odd(even, *halves)

        @pl.when(jnp.logical_not(one | six))
        def _():
            for m in range(4):
                for q in range(8):
                    halves = [weights[g] * coarse[g, 0, m, h, q] for h in range(2)]
                    over_sy[g, m, q] = pack(even, *halves)


def second_kernel(levels, coefficients, coarse, odd, fine, over_sx, corner, rest):
    even = even_lanes()
    weights = [weight_of(coefficients, g) for g in range(2)]

    @pl.loop(0, 2)
    def _(block):
        for k in range(4):
            q = 4 * block + k
            for m in range(3):
                rest[m, q] = added(even, weights, coarse, q, m + 1, 1)

    for g in range(2):
        weight = weight_of(coefficients, g)
        one, four, six = (fine_in(levels, g, which) for which in range(3))

        def nodal(n, m, q):
            return pack(even, *[weight * coarse[g, n, m, h, q] for h in range(2)])

        def each(body):
            @pl.loop(0, 2)
            def _(block):
                for k in range(4):
                    body(4 * block + k)

        @pl.when(one)
        def _():
            def body(q):
                for n in range(2):
                    for m in range(4):
                        halves = []
                        for h in range(2):
                            parents = coarse[g, n, m, h, q]
                            if m < 3:
                                parents = parents + coarse[g, n, m + 1, h, q]
                            halves.append(weight * (odd[0, g, n, m, h, q] - 0.5 * parents))
                        fine[g, m, n, q] = pack(even, *halves)
                    edge = nodal(n, 0, q)
                    over_sx[g, n, q] = edge
                    if n == 0:
                        corner[g, q] = edge

            each(body)

        @pl.when(four)
        def _():
            def body(q):
                for n in range(2):
                    for m in range(4):
                        halves = []
                        for h in range(2):
                            parents = coarse[g, n, m, h, q]
                            if n < 1:
                                parents = parents + coarse[g, n + 1, m, h, q]
                            halves.append(weight * (odd[1, g, n, m, h, q] - 0.5 * parents))
                        packed = pack(even, *halves)
                        fine[g, m, n, q] = packed
                        if m == 0:
                            over_sx[g, n, q] = packed
                corner[g, q] = nodal(0, 0, q)

            each(body)

        @pl.when(six)
        def _():
            def body(q):
                for n in range(2):
                    for m in range(4):
                        halves = [weight * along_lanes(coarse[g, n, m, h, q]) for h in range(2)]
                        packed = pack_odd(even, *halves)
                        fine[g, m, n, q] = packed
                        if m == 0:
                            over_sx[g, n, q] = packed
                            if n == 0:
                                corner[g, q] = packed

            each(body)

        @pl.when(jnp.logical_not(one | four | six))
        def _():
            over_sx[g] = jnp.zeros(over_sx.shape[1:], F32)
            corner[g] = jnp.zeros(corner.shape[1:], F32)


def third_kernel(edge, other_edge, corner, to_sy, to_sx, to_corner):
    for m in range(4):
        to_sy[m] = edge[m] + other_edge[m]
    to_sx[0] = to_sy[0]
    to_sx[1] = edge[4] + other_edge[4]
    to_corner[0] = to_sy[0]
    for g in range(2):
        to_corner[1 + g] = corner[g]


def total(edge, other_edge, rest, other_rest):
    def nodal(q, m, n):
        if n == 0 or m == 0:
            place = m if n == 0 else 4
            return edge[place, q] + other_edge[place, q]
        return rest[m - 1, q] + other_rest[m - 1, q]

    return nodal


def remembered(rule):
    seen = {}

    def value(i, j):
        if (i, j) not in seen:
            seen[i, j] = rule(value, i, j)
        return seen[i, j]

    return value


def mean_pair(x, y):
    return tuple(mean_of(a, b) for a, b in zip(x, y))


def along_one(value, i, j):
    return value(i - 1, j), value(i + 1, j)


def along_four(value, i, j):
    return value(i, j - 1), value(i, j + 1)


def emit(points, late, levels, g, columns, nodal, fine_one, fine_four, fine_six, put, done):
    even = even_lanes()
    one, four, six = (fine_in(levels, g, which) for which in range(3))

    def both(leaf, mean):
        def rule(value, i, j):
            if i % 2:
                return mean(*along_one(value, i, j))
            if j % 2:
                return mean(*along_four(value, i, j))
            return leaf(i // 2, j // 2)

        return remembered(rule)

    def each(row_of):
        @pl.loop(0, 8 // columns)
        def _(block):
            for k in range(columns):
                q = block * columns + k
                row = row_of(q, both(lambda m, n: nodal(q, m, n), mean_of))
                for i, j in points:
                    put(q, i, j, row(i, j))
                done(q)

    @pl.when(one)
    def _():
        def row_of(q, base):
            def extra(value, i, j):
                if j % 2:
                    return mean_of(*along_four(value, i, j))
                return fine_one(q, i // 2, j // 2)

            extra = remembered(extra)

            def rule(value, i, j):
                if j % 2 and not late:
                    return mean_pair(*along_four(value, i, j))
                return expand(even, base(i, j) + extra(i, j) if i % 2 else base(i, j))

            return remembered(rule)

        each(row_of)

    @pl.when(four)
    def _():
        def row_of(q, base):
            def extra(value, i, j):
                if i % 2:
                    return mean_of(*along_one(value, i, j))
                return fine_four(q, i // 2, j // 2)

            extra = remembered(extra)

            def rule(value, i, j):
                if i % 2 and not late:
                    return mean_pair(*along_one(value, i, j))
                return expand(even, base(i, j) + extra(i, j) if j % 2 else base(i, j))

            return remembered(rule)

        each(row_of)

    @pl.when(six)
    def _():
        def row_of(q, base):
            extra = both(lambda m, n: fine_six(q, m, n), mean_of)
            if late:
                return lambda i, j: expand(even, base(i, j), extra(i, j))
            return both(lambda m, n: expand(even, base(2 * m, 2 * n), extra(2 * m, 2 * n)), mean_pair)

        each(row_of)

    @pl.when(jnp.logical_not(one | four | six))
    def _():
        def row_of(q, base):
            if late:
                return lambda i, j: expand(even, base(i, j))
            return both(lambda m, n: expand(even, base(2 * m, 2 * n)), mean_pair)

        each(row_of)


def inner_kernel(levels, edge, other_edge, rest, other_rest, fine, out, held, sem):
    def write(g, q):
        return pltpu.make_async_copy(
            held.at[g, q], out.at[g, pl.ds(0, 7), :, q, pl.ds(0, 3)], sem.at[g, q]
        )

    for g in range(2):

        def put(q, i, j, pair):
            for h in range(2):
                held[g, q, i, h, j] = pair[h]

        def local_fine(q, m, n):
            return fine[g, m, n, q]

        emit(
            [(i, j) for i in range(7) for j in range(3)],
            False,
            levels,
            g,
            4,
            total(edge, other_edge, rest, other_rest),
            local_fine,
            local_fine,
            local_fine,
            put,
            lambda q: write(g, q).start(),
        )
    for g in range(2):
        for q in range(8):
            write(g, q).wait()


def outer_kernel(
    levels,
    edge,
    other_edge,
    rest,
    other_rest,
    fine,
    from_sy,
    from_sx,
    from_corner,
    from_ex,
    fine_sy,
    _,
    out,
    last,
    side,
    sem,
):
    local = total(edge, other_edge, rest, other_rest)

    def writes(g, q):
        return (
            pltpu.make_async_copy(last.at[g, q], out.at[g, 7, :, q], sem.at[0, g, q]),
            pltpu.make_async_copy(
                side.at[g, q], out.at[g, pl.ds(0, 7), :, q, 3], sem.at[1, g, q]
            ),
        )

    def nodal(q, m, n):
        if m < 4 and n < 2:
            return local(q, m, n)
        if m < 4:
            return from_sy[m, q]
        return from_sx[n, q] if n < 2 else from_corner[0, q]

    for g in range(2):

        def put(q, i, j, pair):
            for h in range(2):
                if i == 7:
                    last[g, q, h, j] = pair[h]
                else:
                    side[g, q, i, h] = pair[h]

        def done(q):
            for copy in writes(g, q):
                copy.start()

        def halo_sx(q, n):
            return from_ex[g, n, q]

        def fine_one(q, m, n):
            value = fine[g, m, n, q] if n < 2 else fine_sy[g, m, q]
            if m == 3:
                value = value - 0.5 * (halo_sx(q, n) if n < 2 else from_corner[1 + g, q])
            return value

        def fine_four(q, m, n):
            value = fine[g, m, n, q] if m < 4 else halo_sx(q, n)
            if n == 1:
                value = value - 0.5 * (fine_sy[g, m, q] if m < 4 else from_corner[1 + g, q])
            return value

        def fine_six(q, m, n):
            if m < 4:
                return fine[g, m, n, q] if n < 2 else fine_sy[g, m, q]
            return halo_sx(q, n) if n < 2 else from_corner[1 + g, q]

        emit(
            [(7, j) for j in range(4)] + [(i, 3) for i in range(7)],
            True,
            levels,
            g,
            8,
            nodal,
            fine_one,
            fine_four,
            fine_six,
            put,
            done,
        )
    for g in range(2):
        for q in range(8):
            for copy in writes(g, q):
                copy.wait()


SCALARS = pl.BlockSpec(memory_space=pltpu.SMEM)
WHOLE = pl.BlockSpec(memory_space=pltpu.VMEM)
LEFT = pl.BlockSpec(memory_space=pl.ANY)
FAR = pl.BlockSpec(memory_space=pltpu.HBM)


def shape_of(*leading):
    return jax.ShapeDtypeStruct(leading + TILE, F32)


def held_in(*leading):
    return pltpu.VMEM(leading + TILE, F32)


def params(mebibytes=24):
    return pltpu.CompilerParams(vmem_limit_bytes=mebibytes * 1024 * 1024)


def cost(flops, size):
    return pl.CostEstimate(flops=flops, bytes_accessed=size, transcendentals=0)


def from_next(x, mesh_shape, step, cross=False):
    sizes = [mesh_shape[axis] for axis in AXES]
    pairs = []
    for g in range(sizes[0]):
        for s in range(sizes[1]):
            for y in range(sizes[2]):
                turn = s % 2 if cross else 0
                source = [(c + d) % n for c, d, n in zip((g + turn, s, y), step, sizes)]
                pairs.append(
                    (
                        (source[0] * sizes[1] + source[1]) * sizes[2] + source[2],
                        (g * sizes[1] + s) * sizes[2] + y,
                    )
                )
    return lax.ppermute(x, AXES, pairs)


def local_of(mesh_shape):
    def local(component_grids, levels, coefficients):
        u = component_grids.reshape((2, 4, 2, 2, 8, 2, 2) + TILE)
        edge, over_sy, coarse, odd = pl.pallas_call(
            first_kernel,
            out_shape=(
                shape_of(5, 8),
                shape_of(2, 4, 8),
                shape_of(2, 2, 4, 2, 8),
                shape_of(2, 2, 2, 4, 2, 8),
            ),
            in_specs=[FAR, FAR, FAR],
            out_specs=(WHOLE,) * 4,
            scratch_shapes=[
                pltpu.SMEM((2, 6), jnp.int32),
                pltpu.SMEM((2,), jnp.int32),
                pltpu.SemaphoreType.DMA((14,)),
            ],
            compiler_params=params(),
            cost_estimate=cost(1 << 20, 1 << 21),
            name="first",
        )(*[pltpu.with_memory_space_constraint(x, pltpu.HBM) for x in (levels, coefficients, u)])
        other_edge = from_next(edge, mesh_shape, (1, 0, 0))
        fine_sy = from_next(over_sy, mesh_shape, (0, 0, 1))
        fine, over_sx, corner, rest = pl.pallas_call(
            second_kernel,
            out_shape=(shape_of(2, 4, 2, 8), shape_of(2, 2, 8), shape_of(2, 8), shape_of(3, 8)),
            in_specs=[SCALARS, SCALARS, WHOLE, WHOLE],
            out_specs=(WHOLE,) * 4,
            compiler_params=params(),
            cost_estimate=cost(1 << 20, 1 << 22),
            name="second",
        )(levels, coefficients, coarse, odd)
        other_rest = from_next(rest, mesh_shape, (1, 0, 0))
        to_sy, to_sx, to_corner = pl.pallas_call(
            third_kernel,
            out_shape=(shape_of(4, 8), shape_of(2, 8), shape_of(3, 8)),
            in_specs=[WHOLE] * 3,
            out_specs=(WHOLE,) * 3,
            compiler_params=params(),
            cost_estimate=cost(1 << 16, 1 << 20),
            name="third",
        )(edge, other_edge, corner)
        from_sy = from_next(to_sy, mesh_shape, (0, 0, 1))
        from_ex = from_next(over_sx, mesh_shape, (0, 1, 0))
        from_sx = from_next(to_sx, mesh_shape, (0, 1, 0), cross=True)
        from_corner = from_next(to_corner, mesh_shape, (0, 1, 1))
        parts = (edge, other_edge, rest, other_rest)
        inner = pl.pallas_call(
            inner_kernel,
            out_shape=shape_of(2, 8, 2, 8, 4),
            in_specs=[SCALARS] + [WHOLE] * 5,
            out_specs=LEFT,
            scratch_shapes=[held_in(2, 8, 7, 2, 3), pltpu.SemaphoreType.DMA((2, 8))],
            compiler_params=params(),
            cost_estimate=cost(1 << 20, 1 << 22),
            name="inner",
        )(levels, *parts, fine)
        out = pl.pallas_call(
            outer_kernel,
            out_shape=shape_of(2, 8, 2, 8, 4),
            in_specs=[SCALARS] + [WHOLE] * 10 + [LEFT],
            out_specs=LEFT,
            scratch_shapes=[
                held_in(2, 8, 2, 4),
                held_in(2, 8, 7, 2),
                pltpu.SemaphoreType.DMA((2, 2, 8)),
            ],
            input_output_aliases={11: 0},
            compiler_params=params(),
            cost_estimate=cost(1 << 20, 1 << 22),
            name="outer",
        )(levels, *parts, fine, from_sy, from_sx, from_corner, from_ex, fine_sy, inner)
        return out.reshape(component_grids.shape)

    return local


def solution(mesh):
    return jax.shard_map(
        local_of(dict(mesh.shape)),
        mesh=mesh,
        in_specs=(P("grp", "sx", None, None, "sy", None, None), P("grp", None), P("grp")),
        out_specs=P("grp", "sx", None, None, "sy", None, None),
        check_vma=False,
    )
```

```python
import jax
import jax.numpy as jnp
from jax import lax
from jax.experimental import pallas as pl
from jax.experimental.pallas import tpu as pltpu
from jax.sharding import PartitionSpec as P

AXES = ("grp", "sx", "sy")
FULL = (7, 4, 7)
VARYING = (0, 3, 5)
TILE = (8, 128)
F32 = jnp.float32


def even_lanes():
    return (lax.broadcasted_iota(jnp.int32, TILE, 1) & 1) == 0


def ahead(x, lanes=1):
    return pltpu.roll(x, 128 - lanes, 1)


def behind(x):
    return pltpu.roll(x, 1, 1)


def pack(even, a, b):
    return jnp.where(even, a, behind(b))


def pack_odd(even, a, b):
    return jnp.where(even, ahead(a), b)


def along_lanes(x):
    return x - 0.5 * (behind(x) + ahead(x))


def expand(even, p, odd=None):
    following = ahead(p)
    first, second = 0.5 * (behind(p) + following), 0.5 * (p + ahead(p, 2))
    if odd is not None:
        first, second = first + behind(odd), second + odd
    return jnp.where(even, p, first), jnp.where(even, following, second)


def mean_of(x, y):
    return 0.5 * (x + y)


def fine_in(levels, g, which):
    return levels[g, VARYING[which]] == FULL[which]


def weight_of(coefficients, g):
    return coefficients[g].astype(F32)


def added(even, weights, coarse, q, m, n):
    a, b = (
        weights[0] * coarse[0, n, m, h, q] + weights[1] * coarse[1, n, m, h, q] for h in range(2)
    )
    return pack(even, a, b)


def first_kernel(
    far_levels, far_coefficients, u, edge, over_sy, coarse, odd, levels, coefficients, sem
):
    scalars = [
        pltpu.make_async_copy(far_levels, levels, sem.at[0]),
        pltpu.make_async_copy(far_coefficients, coefficients, sem.at[1]),
    ]
    nodal = [
        pltpu.make_async_copy(u.at[g, :, 0, :, :, n, 0], coarse.at[g, n], sem.at[2 + 2 * g + n])
        for n in range(2)
        for g in range(2)
    ]
    finer = [
        pltpu.make_async_copy(
            u.at[g, :, one, :, :, n, 1 - one], odd.at[1 - one, g, n], sem.at[2 + 4 * (2 - one) + 2 * g + n]
        )
        for one in (1, 0)
        for g in range(2)
        for n in range(2)
    ]
    for copy in scalars + nodal + finer:
        copy.start()
    for copy in scalars:
        copy.wait()
    even = even_lanes()
    weights = [weight_of(coefficients, g) for g in range(2)]
    for copy in nodal[:2]:
        copy.wait()

    @pl.loop(0, 2)
    def _(block):
        for k in range(4):
            q = 4 * block + k
            for m in range(4):
                edge[m, q] = added(even, weights, coarse, q, m, 0)

    for copy in nodal[2:]:
        copy.wait()
    for q in range(8):
        edge[4, q] = added(even, weights, coarse, q, 0, 1)
    for copy in finer:
        copy.wait()
    for g in range(2):
        one, six = fine_in(levels, g, 0), fine_in(levels, g, 2)

        @pl.when(one)
        def _():
            for m in range(4):
                for q in range(8):
                    halves = []
                    for h in range(2):
                        parents = coarse[g, 0, m, h, q]
                        if m < 3:
                            parents = parents + coarse[g, 0, m + 1, h, q]
                        halves.append(weights[g] * (odd[0, g, 0, m, h, q] - 0.5 * parents))
                    over_sy[g, m, q] = pack(even, *halves)

        @pl.when(six)
        def _():
            for m in range(4):
                for q in range(8):
                    halves = [weights[g] * along_lanes(coarse[g, 0, m, h, q]) for h in range(2)]
                    over_sy[g, m, q] = pack_odd(even, *halves)

        @pl.when(jnp.logical_not(one | six))
        def _():
            for m in range(4):
                for q in range(8):
                    halves = [weights[g] * coarse[g, 0, m, h, q] for h in range(2)]
                    over_sy[g, m, q] = pack(even, *halves)


def second_kernel(levels, coefficients, coarse, odd, fine, over_sx, corner, rest):
    even = even_lanes()
    weights = [weight_of(coefficients, g) for g in range(2)]

    @pl.loop(0, 2)
    def _(block):
        for k in range(4):
            q = 4 * block + k
            for m in range(3):
                rest[m, q] = added(even, weights, coarse, q, m + 1, 1)

    for g in range(2):
        weight = weight_of(coefficients, g)
        one, four, six = (fine_in(levels, g, which) for which in range(3))

        def nodal(n, m, q):
            return pack(even, *[weight * coarse[g, n, m, h, q] for h in range(2)])

        def each(body):
            @pl.loop(0, 2)
            def _(block):
                for k in range(4):
                    body(4 * block + k)

        @pl.when(one)
        def _():
            def body(q):
                for n in range(2):
                    for m in range(4):
                        halves = []
                        for h in range(2):
                            parents = coarse[g, n, m, h, q]
                            if m < 3:
                                parents = parents + coarse[g, n, m + 1, h, q]
                            halves.append(weight * (odd[0, g, n, m, h, q] - 0.5 * parents))
                        fine[g, m, n, q] = pack(even, *halves)
                    edge = nodal(n, 0, q)
                    over_sx[g, n, q] = edge
                    if n == 0:
                        corner[g, q] = edge

            each(body)

        @pl.when(four)
        def _():
            def body(q):
                for n in range(2):
                    for m in range(4):
                        halves = []
                        for h in range(2):
                            parents = coarse[g, n, m, h, q]
                            if n < 1:
                                parents = parents + coarse[g, n + 1, m, h, q]
                            halves.append(weight * (odd[1, g, n, m, h, q] - 0.5 * parents))
                        packed = pack(even, *halves)
                        fine[g, m, n, q] = packed
                        if m == 0:
                            over_sx[g, n, q] = packed
                corner[g, q] = nodal(0, 0, q)

            each(body)

        @pl.when(six)
        def _():
            def body(q):
                for n in range(2):
                    for m in range(4):
                        halves = [weight * along_lanes(coarse[g, n, m, h, q]) for h in range(2)]
                        packed = pack_odd(even, *halves)
                        fine[g, m, n, q] = packed
                        if m == 0:
                            over_sx[g, n, q] = packed
                            if n == 0:
                                corner[g, q] = packed

            each(body)

        @pl.when(jnp.logical_not(one | four | six))
        def _():
            over_sx[g] = jnp.zeros(over_sx.shape[1:], F32)
            corner[g] = jnp.zeros(corner.shape[1:], F32)


def third_kernel(edge, other_edge, corner, to_sy, to_sx, to_corner):
    for m in range(4):
        to_sy[m] = edge[m] + other_edge[m]
    to_sx[0] = to_sy[0]
    to_sx[1] = edge[4] + other_edge[4]
    to_corner[0] = to_sy[0]
    for g in range(2):
        to_corner[1 + g] = corner[g]


def total(edge, other_edge, rest, other_rest):
    def nodal(q, m, n):
        if n == 0 or m == 0:
            place = m if n == 0 else 4
            return edge[place, q] + other_edge[place, q]
        return rest[m - 1, q] + other_rest[m - 1, q]

    return nodal


def remembered(rule):
    seen = {}

    def value(i, j):
        if (i, j) not in seen:
            seen[i, j] = rule(value, i, j)
        return seen[i, j]

    return value


def mean_pair(x, y):
    return tuple(mean_of(a, b) for a, b in zip(x, y))


def along_one(value, i, j):
    return value(i - 1, j), value(i + 1, j)


def along_four(value, i, j):
    return value(i, j - 1), value(i, j + 1)


def emit(points, late, levels, g, columns, nodal, fine_one, fine_four, fine_six, put, done):
    even = even_lanes()
    one, four, six = (fine_in(levels, g, which) for which in range(3))

    def both(leaf, mean):
        def rule(value, i, j):
            if i % 2:
                return mean(*along_one(value, i, j))
            if j % 2:
                return mean(*along_four(value, i, j))
            return leaf(i // 2, j // 2)

        return remembered(rule)

    def each(row_of):
        @pl.loop(0, 8 // columns)
        def _(block):
            for k in range(columns):
                q = block * columns + k
                row = row_of(q, both(lambda m, n: nodal(q, m, n), mean_of))
                for i, j in points:
                    put(q, i, j, row(i, j))
                done(q)

    @pl.when(one)
    def _():
        def row_of(q, base):
            def extra(value, i, j):
                if j % 2:
                    return mean_of(*along_four(value, i, j))
                return fine_one(q, i // 2, j // 2)

            extra = remembered(extra)

            def rule(value, i, j):
                if j % 2 and not late:
                    return mean_pair(*along_four(value, i, j))
                return expand(even, base(i, j) + extra(i, j) if i % 2 else base(i, j))

            return remembered(rule)

        each(row_of)

    @pl.when(four)
    def _():
        def row_of(q, base):
            def extra(value, i, j):
                if i % 2:
                    return mean_of(*along_one(value, i, j))
                return fine_four(q, i // 2, j // 2)

            extra = remembered(extra)

            def rule(value, i, j):
                if i % 2 and not late:
                    return mean_pair(*along_one(value, i, j))
                return expand(even, base(i, j) + extra(i, j) if j % 2 else base(i, j))

            return remembered(rule)

        each(row_of)

    @pl.when(six)
    def _():
        def row_of(q, base):
            extra = both(lambda m, n: fine_six(q, m, n), mean_of)
            if late:
                return lambda i, j: expand(even, base(i, j), extra(i, j))
            return both(lambda m, n: expand(even, base(2 * m, 2 * n), extra(2 * m, 2 * n)), mean_pair)

        each(row_of)

    @pl.when(jnp.logical_not(one | four | six))
    def _():
        def row_of(q, base):
            if late:
                return lambda i, j: expand(even, base(i, j))
            return both(lambda m, n: expand(even, base(2 * m, 2 * n)), mean_pair)

        each(row_of)


def inner_kernel(levels, edge, other_edge, rest, other_rest, fine, out, held, sem):
    def write(g, q):
        return pltpu.make_async_copy(
            held.at[g, q], out.at[g, pl.ds(0, 7), :, q, pl.ds(0, 3)], sem.at[g, q]
        )

    for g in range(2):

        def put(q, i, j, pair):
            for h in range(2):
                held[g, q, i, h, j] = pair[h]

        def local_fine(q, m, n):
            return fine[g, m, n, q]

        emit(
            [(i, j) for i in range(7) for j in range(3)],
            False,
            levels,
            g,
            4,
            total(edge, other_edge, rest, other_rest),
            local_fine,
            local_fine,
            local_fine,
            put,
            lambda q: write(g, q).start(),
        )
    for g in range(2):
        for q in range(8):
            write(g, q).wait()


def outer_kernel(
    levels,
    edge,
    other_edge,
    rest,
    other_rest,
    fine,
    from_sy,
    from_sx,
    from_corner,
    from_ex,
    fine_sy,
    _,
    out,
    last,
    side,
    sem,
):
    local = total(edge, other_edge, rest, other_rest)

    def writes(g, q):
        return (
            pltpu.make_async_copy(last.at[g, q], out.at[g, 7, :, q], sem.at[0, g, q]),
            pltpu.make_async_copy(
                side.at[g, q], out.at[g, pl.ds(0, 7), :, q, 3], sem.at[1, g, q]
            ),
        )

    def nodal(q, m, n):
        if m < 4 and n < 2:
            return local(q, m, n)
        if m < 4:
            return from_sy[m, q]
        return from_sx[n, q] if n < 2 else from_corner[0, q]

    for g in range(2):

        def put(q, i, j, pair):
            for h in range(2):
                if i == 7:
                    last[g, q, h, j] = pair[h]
                else:
                    side[g, q, i, h] = pair[h]

        def done(q):
            for copy in writes(g, q):
                copy.start()

        def halo_sx(q, n):
            return from_ex[g, n, q]

        def fine_one(q, m, n):
            value = fine[g, m, n, q] if n < 2 else fine_sy[g, m, q]
            if m == 3:
                value = value - 0.5 * (halo_sx(q, n) if n < 2 else from_corner[1 + g, q])
            return value

        def fine_four(q, m, n):
            value = fine[g, m, n, q] if m < 4 else halo_sx(q, n)
            if n == 1:
                value = value - 0.5 * (fine_sy[g, m, q] if m < 4 else from_corner[1 + g, q])
            return value

        def fine_six(q, m, n):
            if m < 4:
                return fine[g, m, n, q] if n < 2 else fine_sy[g, m, q]
            return halo_sx(q, n) if n < 2 else from_corner[1 + g, q]

        emit(
            [(7, j) for j in range(4)] + [(i, 3) for i in range(7)],
            True,
            levels,
            g,
            8,
            nodal,
            fine_one,
            fine_four,
            fine_six,
            put,
            done,
        )
    for g in range(2):
        for q in range(8):
            for copy in writes(g, q):
                copy.wait()


SCALARS = pl.BlockSpec(memory_space=pltpu.SMEM)
WHOLE = pl.BlockSpec(memory_space=pltpu.VMEM)
LEFT = pl.BlockSpec(memory_space=pl.ANY)
FAR = pl.BlockSpec(memory_space=pltpu.HBM)


def shape_of(*leading):
    return jax.ShapeDtypeStruct(leading + TILE, F32)


def held_in(*leading):
    return pltpu.VMEM(leading + TILE, F32)


def params(mebibytes=24):
    return pltpu.CompilerParams(vmem_limit_bytes=mebibytes * 1024 * 1024)


def cost(flops, size):
    return pl.CostEstimate(flops=flops, bytes_accessed=size, transcendentals=0)


def from_next(x, mesh_shape, step, cross=False):
    sizes = [mesh_shape[axis] for axis in AXES]
    pairs = []
    for g in range(sizes[0]):
        for s in range(sizes[1]):
            for y in range(sizes[2]):
                turn = s % 2 if cross else 0
                source = [(c + d) % n for c, d, n in zip((g + turn, s, y), step, sizes)]
                pairs.append(
                    (
                        (source[0] * sizes[1] + source[1]) * sizes[2] + source[2],
                        (g * sizes[1] + s) * sizes[2] + y,
                    )
                )
    return lax.ppermute(x, AXES, pairs)


def local_of(mesh_shape):
    def local(component_grids, levels, coefficients):
        u = component_grids.reshape((2, 4, 2, 2, 8, 2, 2) + TILE)
        edge, over_sy, coarse, odd = pl.pallas_call(
            first_kernel,
            out_shape=(
                shape_of(5, 8),
                shape_of(2, 4, 8),
                shape_of(2, 2, 4, 2, 8),
                shape_of(2, 2, 2, 4, 2, 8),
            ),
            in_specs=[FAR, FAR, FAR],
            out_specs=(WHOLE,) * 4,
            scratch_shapes=[
                pltpu.SMEM((2, 6), jnp.int32),
                pltpu.SMEM((2,), jnp.int32),
                pltpu.SemaphoreType.DMA((14,)),
            ],
            compiler_params=params(),
            cost_estimate=cost(1 << 20, 1 << 21),
            name="first",
        )(*[pltpu.with_memory_space_constraint(x, pltpu.HBM) for x in (levels, coefficients, u)])
        other_edge = from_next(edge, mesh_shape, (1, 0, 0))
        fine_sy = from_next(over_sy, mesh_shape, (0, 0, 1))
        fine, over_sx, corner, rest = pl.pallas_call(
            second_kernel,
            out_shape=(shape_of(2, 4, 2, 8), shape_of(2, 2, 8), shape_of(2, 8), shape_of(3, 8)),
            in_specs=[SCALARS, SCALARS, WHOLE, WHOLE],
            out_specs=(WHOLE,) * 4,
            compiler_params=params(),
            cost_estimate=cost(1 << 20, 1 << 22),
            name="second",
        )(levels, coefficients, coarse, odd)
        other_rest = from_next(rest, mesh_shape, (1, 0, 0))
        to_sy, to_sx, to_corner = pl.pallas_call(
            third_kernel,
            out_shape=(shape_of(4, 8), shape_of(2, 8), shape_of(3, 8)),
            in_specs=[WHOLE] * 3,
            out_specs=(WHOLE,) * 3,
            compiler_params=params(),
            cost_estimate=cost(1 << 16, 1 << 20),
            name="third",
        )(edge, other_edge, corner)
        from_sy = from_next(to_sy, mesh_shape, (0, 0, 1))
        from_ex = from_next(over_sx, mesh_shape, (0, 1, 0))
        from_sx = from_next(to_sx, mesh_shape, (0, 1, 0), cross=True)
        from_corner = from_next(to_corner, mesh_shape, (0, 1, 1))
        parts = (edge, other_edge, rest, other_rest)
        inner = pl.pallas_call(
            inner_kernel,
            out_shape=shape_of(2, 8, 2, 8, 4),
            in_specs=[SCALARS] + [WHOLE] * 5,
            out_specs=LEFT,
            scratch_shapes=[held_in(2, 8, 7, 2, 3), pltpu.SemaphoreType.DMA((2, 8))],
            compiler_params=params(),
            cost_estimate=cost(1 << 20, 1 << 22),
            name="inner",
        )(levels, *parts, fine)
        out = pl.pallas_call(
            outer_kernel,
            out_shape=shape_of(2, 8, 2, 8, 4),
            in_specs=[SCALARS] + [WHOLE] * 10 + [LEFT],
            out_specs=LEFT,
            scratch_shapes=[
                held_in(2, 8, 2, 4),
                held_in(2, 8, 7, 2),
                pltpu.SemaphoreType.DMA((2, 2, 8)),
            ],
            input_output_aliases={11: 0},
            compiler_params=params(),
            cost_estimate=cost(1 << 20, 1 << 22),
            name="outer",
        )(levels, *parts, fine, from_sy, from_sx, from_corner, from_ex, fine_sy, inner)
        return out.reshape(component_grids.shape)

    return local


def solution(mesh):
    return jax.shard_map(
        local_of(dict(mesh.shape)),
        mesh=mesh,
        in_specs=(P("grp", "sx", None, None, "sy", None, None), P("grp", None), P("grp")),
        out_specs=P("grp", "sx", None, None, "sy", None, None),
        check_vma=False,
    )
```
